32 devices in a mesh: section: 4 (over x, core), dp: 2 (over y), expert: 4 (over z).
Axes of the slice: x: 2, y: 2, z: 4, core: 2. Of those that a mesh axis runs over, the one named last changes fastest.
Arguments:
- incoming: bfloat16 [4, 2, 128, 3584], P('section', None, ('dp', 'expert')), may hold values from -6 to 6
- stash: bfloat16 [4, 2, 128, 3584], P('section', None, ('dp', 'expert')), may hold values from -6 to 6
- expert_ids: int32 [4, 2, 128, 2], P('section', None, ('dp', 'expert')), may hold values from 0 to 3, all different within a row; in each aligned block of 16 rows (0 to 15, 16 to 31, ..., all dimensions but the last counted through in order) at most 12 rows name the same one
- route_weight: float32 [4, 2, 128, 2], P('section', None, ('dp', 'expert')), may hold values from 0.1 to 1
- w_gate: bfloat16 [4, 4, 3584, 2048], P('section', 'expert', None, 'dp'), may hold values from -0.09375 to 0.09375
- w_up: bfloat16 [4, 4, 3584, 2048], P('section', 'expert', None, 'dp'), may hold values from -0.09375 to 0.09375
- w_down: bfloat16 [4, 4, 2048, 3584], P('section', 'expert', 'dp'), may hold values from -0.125 to 0.125
Outputs:
- input_grad: bfloat16 [4, 2, 128, 3584], P('section', None, ('dp', 'expert'))
- grad_gate: bfloat16 [4, 4, 3584, 2048], P('section', 'expert', None, 'dp')
- grad_up: bfloat16 [4, 4, 3584, 2048], P('section', 'expert', None, 'dp')
- grad_down: bfloat16 [4, 4, 2048, 3584], P('section', 'expert', 'dp')
The draws below stay inside these ranges and needn't reach their ends.
Inputs may be any that keep to these rules, and one draw needn't show every extreme that they name: `expert_ids`: each token names 2 different experts. Among the 16 tokens of one device in one micro-batch (aligned blocks of rows), no expert is named by more than 12 of them, a bound that some block reaches.
All inputs are finite; a program needn't handle non-finite values.
Results may differ from the reference program's by a relative error of at most 0.01.
Values may be sent and summed in bfloat16 or wider, within the bound.
A program may use at most 128 MiB of HBM per device.

```python
import math
import jax
import jax.numpy as jnp
import numpy as np
from jax import lax

D = 3584
HID = 2048
TOPK = 2
MB = 2
TOK_DEV = 16
EXPERTS = 4
CAP = 12
TOKENS = 128
N_SECTION = 4
N_DP = 2


def block_scale(own_key, dims, split, low, top_value):
    def one(dim, parts):
        heights = jax.random.uniform(jax.random.fold_in(jax.random.fold_in(own_key, 6), dim), (parts,), jnp.float32, low / len(split), top_value / len(split))
        return jnp.repeat(jnp.exp(heights), dims[dim] // parts).reshape((-1,) + (1,) * (len(dims) - dim - 1))

    loudness = one(*split[0])
    for cut in split[1:]:
        loudness = loudness * one(*cut)
    return loudness


def deal_out(key, own, number, rows, amount, top, limit, skew):
    order = jax.random.permutation(key, amount)
    crowded, common = shares(amount, rows * top, limit, skew, True), shares(amount, rows * top, limit, skew, False)
    places = jnp.arange(amount)

    def named(sizes, offset_by):
        used = int((sizes > 0).sum())
        fixed = max(1, used // 4)
        moved = fixed + (places - fixed + offset_by * (used - fixed)) % max(1, amount - fixed)
        return jnp.zeros((amount,), jnp.int32).at[order[jnp.where(places < fixed, places, moved)]].set(jnp.asarray(sizes, jnp.int32))

    sizes = jnp.where(number % 4 == 0, named(crowded, number // 4), named(common, number - number // 4 - 1))
    mixed = jax.random.permutation(jax.random.fold_in(own, 3), amount)
    donor, taker = mixed[0:amount // 2 * 2:2], mixed[1:amount // 2 * 2:2]
    room = jnp.minimum(sizes[donor] - 1, limit - sizes[taker]) // 2
    room = jnp.where((donor == order[0]) | (taker == order[0]) | (sizes[taker] == 0), 0, jnp.maximum(room, 0))
    moved = jax.random.randint(jax.random.fold_in(own, 4), (amount // 2,), 0, 1 << 20) % (room + 1)
    sizes = sizes.at[donor].add(-moved).at[taker].add(moved)
    items = jnp.searchsorted(jnp.cumsum(sizes), jnp.arange(rows * top), side="right").astype(jnp.int32)
    table = items.reshape(top, rows).T
    table = table[jax.random.permutation(jax.random.fold_in(own, 1), rows)]
    offset_by = jax.random.randint(jax.random.fold_in(own, 2), (rows, 1), 0, top)
    return jnp.take_along_axis(table, (jnp.arange(top)[None, :] + offset_by) % top, axis=1)


def shares(count, total, reach, skew, full):
    weights = [(1 << 20) // math.isqrt(rank ** skew) + 1 for rank in range(1, count + 1)]
    largest = reach if full else min(reach, max(-(-total // count), total * weights[0] // sum(weights)))
    least = 1 if total - largest >= count - 1 else 0
    given, surplus = [largest] + [least] * (count - 1), total - largest - least * (count - 1)
    while surplus > 0:
        movable = [i for i in range(1, count) if given[i] < largest] or [i for i in range(1, count) if given[i] < reach]
        pool, budget = sum([weights[i] for i in movable]), surplus
        for i in movable:
            extra = min(reach - given[i], max(1, budget * weights[i] // pool), surplus)
            given[i] = given[i] + extra
            surplus = surplus - extra
    return np.array(given)


def bell_draw(rng, extent, spread, limit, pieces=(), kind=jnp.bfloat16):
    loudness = block_scale(rng, extent, pieces, -0.22, 0.18) if pieces else 1.0
    result = jax.random.normal(rng, extent, jnp.float32) * spread * loudness
    return jnp.minimum(jnp.maximum(result, -limit), limit).astype(kind)


def setup_inputs(seed: int = 0) -> dict:
    streams_of = jax.random.split(jax.random.key(seed), 8)
    incoming = bell_draw(streams_of[0], (N_SECTION, MB, TOKENS, D), 1.0, 6.0, ((0, 4), (2, 8)))
    stash = bell_draw(streams_of[1], (N_SECTION, MB, TOKENS, D), 1.0, 6.0, ((0, 4), (2, 8)))
    expert_ids_keys = jax.random.split(jax.random.fold_in(streams_of[2], 1), N_SECTION * MB * TOKENS // TOK_DEV)
    expert_ids_turns = jax.random.permutation(jax.random.fold_in(streams_of[2], 3), N_SECTION * MB * TOKENS // TOK_DEV)
    expert_ids = jax.vmap(lambda own, number: deal_out(jax.random.fold_in(streams_of[2], 2), own, number, TOK_DEV, EXPERTS, TOPK, CAP, 2))(expert_ids_keys, expert_ids_turns).reshape((N_SECTION, MB, TOKENS, TOPK))
    route_weight = jnp.clip(0.1 + 0.9 * jax.random.uniform(streams_of[3], (N_SECTION, MB, TOKENS, TOPK), jnp.float32) ** block_scale(streams_of[3], (N_SECTION, MB, TOKENS, TOPK), ((0, 4), (2, 8)), -0.2, 0.2), 0.1, 1.0)
    w_gate = bell_draw(streams_of[4], (N_SECTION, EXPERTS, D, HID), D ** -0.5, 0.09375, ((0, 4), (1, 4), (3, 2)))
    w_up = bell_draw(streams_of[5], (N_SECTION, EXPERTS, D, HID), D ** -0.5, 0.09375, ((0, 4), (1, 4), (3, 2)))
    w_down = bell_draw(streams_of[6], (N_SECTION, EXPERTS, HID, D), HID ** -0.5, 0.125, ((0, 4), (1, 4), (2, 2)))
    return dict(incoming=incoming, stash=stash, expert_ids=expert_ids, route_weight=route_weight, w_gate=w_gate, w_up=w_up, w_down=w_down)


def reference(incoming, stash, expert_ids, route_weight, w_gate, w_up, w_down):
    upstream_all = jnp.roll(incoming, -1, axis=0)
    groups = N_DP * EXPERTS
    pair_count = TOK_DEV * TOPK
    block_width = HID // N_DP
    row_total = MB * groups * CAP
    batch_index = jnp.arange(MB, dtype=jnp.int32)[:, None, None]
    group_index = jnp.arange(groups, dtype=jnp.int32)[None, :, None]
    input_grads = []
    gate_sections = []
    up_sections = []
    down_sections = []
    for section_index in range(N_SECTION):
        upstream = upstream_all[section_index].reshape(MB, groups, TOK_DEV, D)
        tokens = stash[section_index].reshape(MB, groups, TOK_DEV, D)
        chosen = expert_ids[section_index].reshape(MB, groups, pair_count).astype(jnp.int32)
        weight_pairs = route_weight[section_index].reshape(MB, groups, pair_count)
        onehot = (chosen[..., None] == jnp.arange(EXPERTS, dtype=jnp.int32)).astype(jnp.int32)
        running = jnp.cumsum(onehot, axis=2).astype(jnp.int32) - 1
        position = jnp.sum(onehot * running, axis=3).astype(jnp.int32)
        slot_index = (chosen * CAP + position).astype(jnp.int32)
        pair_inputs = jnp.repeat(tokens, TOPK, axis=2)
        pair_scaled = (weight_pairs[..., None] * jnp.repeat(upstream, TOPK, axis=2).astype(jnp.float32)).astype(jnp.bfloat16)
        empty_slots = jnp.zeros((MB, groups, EXPERTS * CAP, D), jnp.bfloat16)
        input_slots = empty_slots.at[batch_index, group_index, slot_index].set(pair_inputs).reshape(MB, groups, EXPERTS, CAP, D)
        scaled_slots = empty_slots.at[batch_index, group_index, slot_index].set(pair_scaled).reshape(MB, groups, EXPERTS, CAP, D)
        backs = []
        gate_experts = []
        up_experts = []
        down_experts = []
        for expert_index in range(EXPERTS):
            input_rows = input_slots[:, :, expert_index].reshape(row_total, D)
            scaled_rows = scaled_slots[:, :, expert_index].reshape(row_total, D)
            gate_full = w_gate[section_index, expert_index]
            up_full = w_up[section_index, expert_index]
            down_full = w_down[section_index, expert_index]
            gate_pre = jnp.dot(input_rows, gate_full, preferred_element_type=jnp.float32)
            up_pre = jnp.dot(input_rows, up_full, preferred_element_type=jnp.float32)
            logistic = jax.nn.sigmoid(gate_pre)
            activated = gate_pre * logistic
            hidden = (activated * up_pre).astype(jnp.bfloat16)
            hidden_grad = jnp.dot(scaled_rows, down_full.T, preferred_element_type=jnp.float32)
            gate_grad = (hidden_grad * up_pre * logistic * (1.0 + gate_pre * (1.0 - logistic))).astype(jnp.bfloat16)
            up_grad = (hidden_grad * activated).astype(jnp.bfloat16)
            down_experts.append(jnp.dot(hidden.T, scaled_rows, preferred_element_type=jnp.float32).astype(jnp.bfloat16))
            gate_experts.append(jnp.dot(input_rows.T, gate_grad, preferred_element_type=jnp.float32).astype(jnp.bfloat16))
            up_experts.append(jnp.dot(input_rows.T, up_grad, preferred_element_type=jnp.float32).astype(jnp.bfloat16))
            gate_blocks = gate_grad.astype(jnp.float32).reshape(row_total, N_DP, block_width)
            up_blocks = up_grad.astype(jnp.float32).reshape(row_total, N_DP, block_width)
            gate_weights = gate_full.astype(jnp.float32).reshape(D, N_DP, block_width)
            up_weights = up_full.astype(jnp.float32).reshape(D, N_DP, block_width)
            partial_value = jnp.einsum("rnh,dnh->rnd", gate_blocks, gate_weights) + jnp.einsum("rnh,dnh->rnd", up_blocks, up_weights)
            rounded = lax.optimization_barrier(partial_value.astype(jnp.bfloat16)).astype(jnp.float32)
            pair_back = lax.optimization_barrier(jnp.sum(rounded, axis=1).astype(jnp.bfloat16))
            backs.append(pair_back.reshape(MB, groups, CAP, D))
        back_slots = jnp.stack(backs, axis=2).reshape(MB, groups, EXPERTS * CAP, D)
        per_pair = back_slots[batch_index, group_index, slot_index].astype(jnp.float32).reshape(MB, groups, TOK_DEV, TOPK, D)
        section_grad = (upstream.astype(jnp.float32) + jnp.sum(per_pair, axis=3)).astype(jnp.bfloat16)
        input_grads.append(section_grad.reshape(MB, groups * TOK_DEV, D))
        gate_sections.append(jnp.stack(gate_experts))
        up_sections.append(jnp.stack(up_experts))
        down_sections.append(jnp.stack(down_experts))
    return (jnp.stack(input_grads), jnp.stack(gate_sections), jnp.stack(up_sections), jnp.stack(down_sections))
```

```python
import jax
import jax.numpy as jnp
from jax import lax
from jax.sharding import PartitionSpec as P


def passed_along(x, axis, by):
    length = lax.axis_size(axis)
    return lax.ppermute(x, axis, [(i, (i + by) % length) for i in range(length)])


def per_device(incoming, stash, expert_ids, route_weight, w_gate, w_up, w_down):
    group = ("dp", "expert")
    mbatch, tok_rows, width = stash.shape[1:]
    rows = mbatch * tok_rows
    mine = lax.axis_index("expert")
    own_tokens = stash[0].reshape(rows, width)
    upstream = passed_along(incoming[0].reshape(rows, width), "section", -1)
    experts = lax.axis_size("expert")
    named = expert_ids[0][..., None] == jnp.arange(experts, dtype=jnp.int32)
    token_weight = jnp.sum(
        jnp.where(named, route_weight[0][..., None], 0.0), axis=2
    ).reshape(rows, experts)
    all_weight = lax.all_gather(token_weight, group, axis=0, tiled=True)
    tokens = lax.all_gather(own_tokens, group, axis=0, tiled=True)
    ups = lax.all_gather(upstream, group, axis=0, tiled=True)
    weight = lax.dynamic_slice_in_dim(all_weight, mine, 1, axis=1)
    gate_slice, up_slice, down_slice = w_gate[0, 0], w_up[0, 0], w_down[0, 0]
    contract_rows = (((0,), (0,)), ((), ()))
    contract_last = (((1,), (1,)), ((), ()))
    f32 = jnp.float32
    gate_pre = jnp.dot(tokens, gate_slice, preferred_element_type=f32)
    up_pre = jnp.dot(tokens, up_slice, preferred_element_type=f32)
    logistic = jax.nn.sigmoid(gate_pre)
    activated = gate_pre * logistic
    hidden = (activated * up_pre).astype(jnp.bfloat16)
    scaled = (weight * ups.astype(f32)).astype(jnp.bfloat16)
    hidden_grad = lax.dot_general(scaled, down_slice, contract_last, preferred_element_type=f32)
    gate_grad = (hidden_grad * up_pre * logistic * (1.0 + gate_pre * (1.0 - logistic))).astype(
        jnp.bfloat16
    )
    up_grad = (hidden_grad * activated).astype(jnp.bfloat16)
    back = lax.dot_general(gate_grad, gate_slice, contract_last, preferred_element_type=f32)
    back = back + lax.dot_general(up_grad, up_slice, contract_last, preferred_element_type=f32)
    summed = lax.psum_scatter(
        back.astype(jnp.bfloat16), group, scatter_dimension=0, tiled=True
    )
    grad_down = lax.dot_general(hidden, scaled, contract_rows, preferred_element_type=f32)
    grad_gate = lax.dot_general(tokens, gate_grad, contract_rows, preferred_element_type=f32)
    grad_up = lax.dot_general(tokens, up_grad, contract_rows, preferred_element_type=f32)
    input_grad = (upstream.astype(f32) + summed.astype(f32)).astype(jnp.bfloat16)
    return (
        input_grad.reshape(1, mbatch, tok_rows, width),
        grad_gate.astype(jnp.bfloat16)[None, None],
        grad_up.astype(jnp.bfloat16)[None, None],
        grad_down.astype(jnp.bfloat16)[None, None],
    )


def solution(mesh):
    tokens = P("section", None, ("dp", "expert"), None)
    columns = P("section", "expert", None, "dp")
    rows = P("section", "expert", "dp", None)
    return jax.shard_map(
        per_device,
        mesh=mesh,
        in_specs=(tokens, tokens, tokens, tokens, columns, columns, rows),
        out_specs=(tokens, columns, columns, rows),
        check_vma=False,
    )
```

```python
import functools

import jax
import jax.numpy as jnp
from jax import lax
from jax.experimental import pallas as pl
from jax.experimental.pallas import tpu as pltpu
from jax.sharding import PartitionSpec as P

F32 = jnp.float32
BF16 = jnp.bfloat16
LAST = (((1,), (1,)), ((), ()))
FIRST = (((0,), (0,)), ((), ()))
VMEM_LIMIT = 60 * 1024 * 1024
CHUNKS = 2


def exchange_kernel(sizes, *refs):
    sections, replicas, experts = sizes
    (incoming, stash, weight, gate_hbm, up_hbm, down_hbm), refs = refs[:6], refs[6:]
    (own_up, hidden_ref, gate_grad_ref, up_grad_ref, x_out, s_out), refs = refs[:6], refs[6:]
    parts, refs = refs[: CHUNKS * replicas], refs[CHUNKS * replicas :]
    (xbuf, ubuf, wbuf, gate_w, up_w, down_w, gate_pre, up_pre) = refs[:8]
    (load_sem, out_sem, part_sem, shift_send, shift_recv, w_send, w_recv, zsend, dsend, recv) = refs[8:]
    groups, rows, width = xbuf.shape
    hid = gate_w.shape[1]
    tile = min(256, hid)
    tiles = hid // tile
    per_block = max(1, min(groups, 256 // rows))
    blocks = groups // per_block
    height = per_block * rows
    s, d, e = lax.axis_index("section"), lax.axis_index("dp"), lax.axis_index("expert")
    cut = (width // 128) * 17 // 28 * 128
    columns = (pl.ds(0, cut), pl.ds(cut, width - cut))

    def slot(replica, expert):
        return lax.rem(replica + replicas, replicas) * experts + jnp.clip(expert, 0, experts - 1)

    me = slot(d, e)
    loads = [
        pltpu.make_async_copy(src, dst, load_sem.at[i])
        for i, (src, dst) in enumerate(((gate_hbm, gate_w), (up_hbm, up_w), (down_hbm, down_w)))
    ]
    peers = [(j, k) for j in range(replicas) for k in range(experts) if j or k]

    def peer(j, k):
        return {"dp": lax.rem(d + j, replicas), "expert": lax.rem(e + k, experts)}

    before = {"section": lax.rem(s + sections - 1, sections)}
    after = {"section": lax.rem(s + 1, sections)}
    barrier = pltpu.get_barrier_semaphore()
    for target in [peer(j, k) for j, k in peers] + [before, after]:
        pl.semaphore_signal(barrier, inc=1, device_id=target, device_id_type=pl.DeviceIdType.MESH)
    xbuf[me] = stash[...]
    wbuf[me] = weight[...]
    pl.semaphore_wait(barrier, len(peers) + 2)

    def remote(src, dst, send, arrive, target):
        return pltpu.make_async_remote_copy(
            src_ref=src,
            dst_ref=dst,
            send_sem=send,
            recv_sem=arrive,
            device_id=target,
            device_id_type=pl.DeviceIdType.MESH,
        )

    bufs = (xbuf, ubuf)

    def along_z(a, c, block, way):
        ref = bufs[a].at[block, :, columns[c]]
        other = jnp.clip(e + 1 if way == 0 else e - 1, 0, experts - 1)
        return remote(ref, ref, zsend.at[a, c, way, block], recv.at[a, c, block], {"expert": other})

    def along_dp(a, c, expert, j):
        block = slot(d, expert)
        ref = bufs[a].at[block, :, columns[c]]
        at = jnp.clip(expert, 0, experts - 1)
        return remote(ref, ref, dsend.at[a, c, j - 1, at], recv.at[a, c, block], peer(j, 0))

    def arrived(a, c, block):
        ref = bufs[a].at[block, :, columns[c]]
        remote(ref, ref, zsend.at[a, c, 0, block], recv.at[a, c, block], peer(1, 0)).wait_recv()

    others = range(1, replicas)
    has = (e < experts - 1, e > 0)

    def both_ways(a, c, block):
        for way in range(2):
            pl.when(has[way])(lambda way=way: along_z(a, c, block, way).start())

    def first(a):
        for j in others:
            along_dp(a, 1, e, j).start()
        both_ways(a, 0, me)
        for j in others:
            along_dp(a, 0, e, j).start()
        both_ways(a, 1, me)

    def relay(a, c, replica, k, with_dp):
        for way, origin, there in ((0, e - k, e - k >= 0), (1, e + k, e + k < experts)):

            @pl.when(there)
            def _():
                block = slot(replica, origin)
                arrived(a, c, block)
                pl.when(has[way])(lambda: along_z(a, c, block, way).start())
                if with_dp:
                    for j in others:
                        along_dp(a, c, origin, j).start()

    def step(a, k):
        relay(a, 0, d, k, True)
        for j in others:
            if k == 1:
                arrived(a, 1, slot(d - j, e))
                both_ways(a, 1, slot(d - j, e))
            else:
                relay(a, 1, d - j, k - 1, False)
        relay(a, 1, d, k, False)

    def finish(a):
        for j in others:
            relay(a, 1, d - j, experts - 1, False)
            for expert in range(experts):
                arrived(a, 0, slot(d - j, expert))

    def sent(a):
        for c in range(2):
            for j in others:
                for expert in range(experts):
                    if c == 0:
                        along_dp(a, 0, expert, j).wait_send()
                if c == 1:
                    along_dp(a, 1, e, j).wait_send()
            for j in range(replicas if c == 1 else 1):
                for k in range(experts):
                    for way, origin, there in ((0, e - k, e - k >= 0), (1, e + k, e + k < experts)):

                        @pl.when(jnp.logical_and(there, has[way]))
                        def _():
                            along_z(a, c, slot(d - j, origin), way).wait_send()

    shift = remote(incoming, ubuf.at[me], shift_send.at[0], shift_recv.at[0], before)
    shift.start()
    first(0)
    weight_copies = []
    for n, (j, k) in enumerate(peers):
        copy = remote(wbuf.at[me], wbuf.at[me], w_send.at[n], w_recv.at[n], peer(j, k))
        copy.start()
        weight_copies.append(copy)
    for load in loads:
        load.start()
    shift.wait()
    own_up[...] = ubuf[me]
    first(1)
    for k in range(1, experts):
        step(0, k)
    finish(0)
    x_copy = pltpu.make_async_copy(xbuf, x_out, out_sem.at[0])
    x_copy.start()
    loads[0].wait()
    loads[1].wait()

    def forward(lo, hi):
        @pl.loop(lo, hi)
        def _(h):
            cols = pl.ds(pl.multiple_of(h * tile, tile), tile)

            @pl.loop(0, blocks)
            def _(r):
                x = xbuf[pl.ds(r * per_block, per_block)].reshape(height, width)
                gate_pre[h, r] = jnp.dot(x, gate_w[:, cols], preferred_element_type=F32)
                up_pre[h, r] = jnp.dot(x, up_w[:, cols], preferred_element_type=F32)

    for k in range(1, experts):
        step(1, k)
        lo, hi = tiles * (k - 1) // (experts - 1), tiles * k // (experts - 1)
        if hi > lo:
            forward(lo, hi)
    finish(1)
    for copy in weight_copies:
        copy.wait()
    sent(1)
    lane = lax.broadcasted_iota(jnp.int32, wbuf.shape[1:], 1)

    @pl.loop(0, groups)
    def _(g):
        own = jnp.sum(jnp.where(lane == e, wbuf[g], 0.0), axis=1, keepdims=True)
        ubuf[g] = (own * ubuf[g].astype(F32)).astype(BF16)

    s_copy = pltpu.make_async_copy(ubuf, s_out, out_sem.at[1])
    s_copy.start()
    loads[2].wait()

    @pl.loop(0, tiles)
    def _(h):
        cols = pl.ds(pl.multiple_of(h * tile, tile), tile)

        @pl.loop(0, blocks)
        def _(r):
            at = pl.ds(pl.multiple_of(r * height, height), height)
            scaled = ubuf[pl.ds(r * per_block, per_block)].reshape(height, width)
            grad = lax.dot_general(scaled, down_w[cols, :], LAST, preferred_element_type=F32)
            gate, up = gate_pre[h, r], up_pre[h, r]
            logistic = jax.nn.sigmoid(gate)
            active = gate * logistic
            hidden_ref[at, cols] = (active * up).astype(BF16)
            gate_grad_ref[at, cols] = (
                grad * up * logistic * (1.0 + gate * (1.0 - logistic))
            ).astype(BF16)
            up_grad_ref[at, cols] = (grad * active).astype(BF16)

    sent(0)
    x_copy.wait()
    piece = width // CHUNKS
    sub = 256
    copies = []
    for c in range(CHUNKS):

        @pl.loop(0, piece // sub)
        def _(t):
            cols = pl.ds(pl.multiple_of(c * piece + t * sub, sub), sub)

            @pl.loop(0, blocks)
            def _(r):
                at = pl.ds(pl.multiple_of(r * height, height), height)
                back = lax.dot_general(
                    gate_grad_ref[at, :], gate_w[cols, :], LAST, preferred_element_type=F32
                ) + lax.dot_general(
                    up_grad_ref[at, :], up_w[cols, :], LAST, preferred_element_type=F32
                )
                xbuf[pl.ds(r * per_block, per_block), :, cols] = back.astype(BF16).reshape(
                    per_block, rows, sub
                )

        for j in range(replicas):
            for k in range(experts):
                copy = pltpu.make_async_copy(
                    xbuf.at[slot(d + j, lax.rem(e + k, experts)), :, pl.ds(c * piece, piece)],
                    parts[c * replicas + j].at[k],
                    part_sem.at[c, j, k],
                )
                copy.start()
                copies.append(copy)
    for copy in copies:
        copy.wait()
    s_copy.wait()


def exchange(sizes, incoming, stash, weight, gate, up, down):
    _, replicas, experts = sizes
    groups = replicas * experts
    rows, width = stash.shape
    hid = gate.shape[1]
    total = groups * rows
    tile = min(256, hid)
    per_block = max(1, min(groups, 256 // rows))
    dma = pltpu.SemaphoreType.DMA
    vmem, anywhere = pl.BlockSpec(memory_space=pltpu.VMEM), pl.BlockSpec(memory_space=pl.ANY)
    shape = jax.ShapeDtypeStruct
    pre = pltpu.VMEM((hid // tile, groups // per_block, per_block * rows, tile), F32)
    tokens = pltpu.VMEM((groups, rows, width), BF16)
    return pl.pallas_call(
        functools.partial(exchange_kernel, sizes),
        out_shape=[shape((rows, width), BF16)]
        + [shape((total, hid), BF16)] * 3
        + [shape((groups, rows, width), BF16)] * 2
        + [shape((experts, rows, width // CHUNKS), BF16)] * (CHUNKS * replicas),
        in_specs=[vmem] * 3 + [anywhere] * 3,
        out_specs=[vmem] * 4 + [anywhere] * (2 + CHUNKS * replicas),
        scratch_shapes=[
            tokens,
            tokens,
            pltpu.VMEM((groups, rows, 128), F32),
            pltpu.VMEM(gate.shape, BF16),
            pltpu.VMEM(up.shape, BF16),
            pltpu.VMEM(down.shape, BF16),
            pre,
            pre,
            dma((3,)),
            dma((2,)),
            dma((CHUNKS, replicas, experts)),
            dma((1,)),
            dma((1,)),
            dma((groups - 1,)),
            dma((groups - 1,)),
            dma((2, 2, 2, groups)),
            dma((2, 2, max(1, replicas - 1), experts)),
            dma((2, 2, groups)),
        ],
        compiler_params=pltpu.CompilerParams(
            collective_id=0, has_side_effects=True, vmem_limit_bytes=VMEM_LIMIT
        ),
        cost_estimate=pl.CostEstimate(
            flops=10 * total * width * hid, bytes_accessed=6 * width * hid, transcendentals=0
        ),
    )(incoming, stash, weight, gate, up, down)


def outer_kernel(lhs, *refs):
    half = len(refs) // 2
    for rhs, out in zip(refs[:half], refs[half:]):
        out[...] = lax.dot_general(lhs[...], rhs[...], FIRST, preferred_element_type=F32).astype(
            BF16
        )


def outer(lhs, tile, *rhs):
    total, height = lhs.shape
    out_width = rhs[0].shape[1]
    tile = min(tile, height)
    return pl.pallas_call(
        outer_kernel,
        grid=(height // tile,),
        in_specs=[pl.BlockSpec((total, tile), lambda i: (0, i))]
        + [pl.BlockSpec((total, out_width), lambda i: (0, 0))] * len(rhs),
        out_specs=[pl.BlockSpec((tile, out_width), lambda i: (i, 0))] * len(rhs),
        out_shape=[jax.ShapeDtypeStruct((height, out_width), BF16)] * len(rhs),
        compiler_params=pltpu.CompilerParams(vmem_limit_bytes=50 * 1024 * 1024),
        cost_estimate=pl.CostEstimate(
            flops=2 * total * height * out_width * len(rhs),
            bytes_accessed=2 * len(rhs) * height * out_width,
            transcendentals=0,
        ),
    )(lhs, *rhs)


def passed_along(x, axis, by):
    length = lax.axis_size(axis)
    return lax.ppermute(x, axis, [(i, (i + by) % length) for i in range(length)])


def per_device(sizes, incoming, stash, expert_ids, route_weight, w_gate, w_up, w_down):
    _, replicas, experts = sizes
    mbatch, tok_rows, width = stash.shape[1:]
    rows = mbatch * tok_rows
    named = expert_ids[0][..., None] == jnp.arange(128, dtype=jnp.int32)
    weight = jnp.sum(jnp.where(named, route_weight[0][..., None], 0.0), axis=2).reshape(rows, 128)
    outs = exchange(
        sizes,
        incoming[0].reshape(rows, width),
        stash[0].reshape(rows, width),
        weight,
        w_gate[0, 0],
        w_up[0, 0],
        w_down[0, 0],
    )
    upstream, hidden, gate_grad, up_grad, tokens, scaled = outs[:6]
    parts = outs[6:]
    tokens = tokens.reshape(-1, width)
    scaled = scaled.reshape(-1, width)
    summed = []
    for c in range(CHUNKS):
        mine = parts[c * replicas : (c + 1) * replicas]
        total = mine[0].astype(F32)
        for j in range(1, replicas):
            total = total + passed_along(mine[j], "dp", j).astype(F32)
        total = total.astype(BF16)
        back = total[0].astype(F32)
        for k in range(1, experts):
            back = back + passed_along(total[k], "expert", k).astype(F32)
        summed.append(back)
    grad_gate, grad_up = outer(tokens, 512, gate_grad, up_grad)
    (grad_down,) = outer(hidden, 256, scaled)
    input_grad = (upstream.astype(F32) + jnp.concatenate(summed, axis=1)).astype(BF16)
    return (
        input_grad.reshape(1, mbatch, tok_rows, width),
        grad_gate[None, None],
        grad_up[None, None],
        grad_down[None, None],
    )


def solution(mesh):
    sizes = tuple(mesh.shape[name] for name in ("section", "dp", "expert"))
    tokens = P("section", None, ("dp", "expert"), None)
    columns = P("section", "expert", None, "dp")
    rows = P("section", "expert", "dp", None)
    return jax.shard_map(
        functools.partial(per_device, sizes),
        mesh=mesh,
        in_specs=(tokens, tokens, tokens, tokens, columns, columns, rows),
        out_specs=(tokens, columns, columns, rows),
        check_vma=False,
    )
```

```python
import functools

import jax
import jax.numpy as jnp
from jax import lax
from jax.experimental import pallas as pl
from jax.experimental.pallas import tpu as pltpu
from jax.sharding import PartitionSpec as P

F32 = jnp.float32
BF16 = jnp.bfloat16
LAST = (((1,), (1,)), ((), ()))
FIRST = (((0,), (0,)), ((), ()))
VMEM_LIMIT = 60 * 1024 * 1024
CHUNKS = 7


def exchange_kernel(sizes, *refs):
    sections, replicas, experts = sizes
    (incoming, stash, weight, gate_hbm, up_hbm, down_hbm), refs = refs[:6], refs[6:]
    (own_up, hidden_ref, gate_grad_ref, up_grad_ref, x_out, s_out), refs = refs[:6], refs[6:]
    (xbuf, ubuf, wbuf, back_buf, gate_w, up_w, down_w, gate_pre, up_pre) = refs[:9]
    (load_sem, out_sem, shift_send, shift_recv, w_send, w_recv, zsend, dsend, recv) = refs[9:18]
    (ready, y_send, y_recv, z_send, z_recv) = refs[18:]
    groups, rows, width = xbuf.shape
    hid = gate_w.shape[1]
    tile = min(256, hid)
    tiles = hid // tile
    per_block = max(1, min(groups, 256 // rows))
    blocks = groups // per_block
    height = per_block * rows
    s, d, e = lax.axis_index("section"), lax.axis_index("dp"), lax.axis_index("expert")
    cut = (width // 128) * 17 // 28 * 128
    columns = (pl.ds(0, cut), pl.ds(cut, width - cut))

    def slot(replica, expert):
        return lax.rem(replica + replicas, replicas) * experts + jnp.clip(expert, 0, experts - 1)

    me = slot(d, e)
    loads = [
        pltpu.make_async_copy(src, dst, load_sem.at[i])
        for i, (src, dst) in enumerate(((gate_hbm, gate_w), (up_hbm, up_w), (down_hbm, down_w)))
    ]
    peers = [(j, k) for j in range(replicas) for k in range(experts) if j or k]

    def peer(j, k):
        return {"dp": lax.rem(d + j, replicas), "expert": lax.rem(e + k, experts)}

    before = {"section": lax.rem(s + sections - 1, sections)}
    after = {"section": lax.rem(s + 1, sections)}
    barrier = pltpu.get_barrier_semaphore()
    for target in [peer(j, k) for j, k in peers] + [before, after]:
        pl.semaphore_signal(barrier, inc=1, device_id=target, device_id_type=pl.DeviceIdType.MESH)
    xbuf[me] = stash[...]
    wbuf[me] = weight[...]
    pl.semaphore_wait(barrier, len(peers) + 2)

    def remote(src, dst, send, arrive, target):
        return pltpu.make_async_remote_copy(
            src_ref=src,
            dst_ref=dst,
            send_sem=send,
            recv_sem=arrive,
            device_id=target,
            device_id_type=pl.DeviceIdType.MESH,
        )

    bufs = (xbuf, ubuf)

    def along_z(a, c, block, way):
        ref = bufs[a].at[block, :, columns[c]]
        other = jnp.clip(e + 1 if way == 0 else e - 1, 0, experts - 1)
        return remote(ref, ref, zsend.at[a, c, way, block], recv.at[a, c, block], {"expert": other})

    def along_dp(a, c, expert, j):
        block = slot(d, expert)
        ref = bufs[a].at[block, :, columns[c]]
        at = jnp.clip(expert, 0, experts - 1)
        return remote(ref, ref, dsend.at[a, c, j - 1, at], recv.at[a, c, block], peer(j, 0))

    def arrived(a, c, block):
        ref = bufs[a].at[block, :, columns[c]]
        remote(ref, ref, zsend.at[a, c, 0, block], recv.at[a, c, block], peer(1, 0)).wait_recv()

    others = range(1, replicas)
    has = (e < experts - 1, e > 0)

    def both_ways(a, c, block):
        for way in range(2):
            pl.when(has[way])(lambda way=way: along_z(a, c, block, way).start())

    def first(a):
        for j in others:
            along_dp(a, 1, e, j).start()
        both_ways(a, 0, me)
        for j in others:
            along_dp(a, 0, e, j).start()
        both_ways(a, 1, me)

    def relay(a, c, replica, k, with_dp):
        for way, origin, there in ((0, e - k, e - k >= 0), (1, e + k, e + k < experts)):

            @pl.when(there)
            def _():
                block = slot(replica, origin)
                arrived(a, c, block)
                pl.when(has[way])(lambda: along_z(a, c, block, way).start())
                if with_dp:
                    for j in others:
                        along_dp(a, c, origin, j).start()

    def step(a, k):
        relay(a, 0, d, k, True)
        for j in others:
            if k == 1:
                arrived(a, 1, slot(d - j, e))
                both_ways(a, 1, slot(d - j, e))
            else:
                relay(a, 1, d - j, k - 1, False)
        relay(a, 1, d, k, False)

    def finish(a):
        for j in others:
            relay(a, 1, d - j, experts - 1, False)
            for expert in range(experts):
                arrived(a, 0, slot(d - j, expert))

    def sent(a):
        for c in range(2):
            for j in others:
                for expert in range(experts):
                    if c == 0:
                        along_dp(a, 0, expert, j).wait_send()
                if c == 1:
                    along_dp(a, 1, e, j).wait_send()
            for j in range(replicas if c == 1 else 1):
                for k in range(experts):
                    for way, origin, there in ((0, e - k, e - k >= 0), (1, e + k, e + k < experts)):

                        @pl.when(jnp.logical_and(there, has[way]))
                        def _():
                            along_z(a, c, slot(d - j, origin), way).wait_send()

    shift = remote(incoming, ubuf.at[me], shift_send.at[0], shift_recv.at[0], before)
    shift.start()
    first(0)
    weight_copies = []
    for n, (j, k) in enumerate(peers):
        copy = remote(wbuf.at[me], wbuf.at[me], w_send.at[n], w_recv.at[n], peer(j, k))
        copy.start()
        weight_copies.append(copy)
    for load in loads:
        load.start()
    shift.wait()
    own_up[...] = ubuf[me]
    first(1)
    for k in range(1, experts):
        step(0, k)
    finish(0)
    x_copy = pltpu.make_async_copy(xbuf, x_out, out_sem.at[0])
    x_copy.start()
    loads[0].wait()
    loads[1].wait()

    def forward(lo, hi):
        @pl.loop(lo, hi)
        def _(h):
            cols = pl.ds(pl.multiple_of(h * tile, tile), tile)

            @pl.loop(0, blocks)
            def _(r):
                x = xbuf[pl.ds(r * per_block, per_block)].reshape(height, width)
                gate_pre[h, r] = jnp.dot(x, gate_w[:, cols], preferred_element_type=F32)
                up_pre[h, r] = jnp.dot(x, up_w[:, cols], preferred_element_type=F32)

    for k in range(1, experts):
        step(1, k)
        lo, hi = tiles * (k - 1) // (experts - 1), tiles * k // (experts - 1)
        if hi > lo:
            forward(lo, hi)
    finish(1)
    for copy in weight_copies:
        copy.wait()
    sent(1)
    lane = lax.broadcasted_iota(jnp.int32, wbuf.shape[1:], 1)

    @pl.loop(0, groups)
    def _(g):
        own = jnp.sum(jnp.where(lane == e, wbuf[g], 0.0), axis=1, keepdims=True)
        ubuf[g] = (own * ubuf[g].astype(F32)).astype(BF16)

    s_copy = pltpu.make_async_copy(ubuf, s_out, out_sem.at[1])
    s_copy.start()
    loads[2].wait()

    @pl.loop(0, tiles)
    def _(h):
        cols = pl.ds(pl.multiple_of(h * tile, tile), tile)

        @pl.loop(0, blocks)
        def _(r):
            at = pl.ds(pl.multiple_of(r * height, height), height)
            scaled = ubuf[pl.ds(r * per_block, per_block)].reshape(height, width)
            grad = lax.dot_general(scaled, down_w[cols, :], LAST, preferred_element_type=F32)
            gate, up = gate_pre[h, r], up_pre[h, r]
            logistic = jax.nn.sigmoid(gate)
            active = gate * logistic
            hidden_ref[at, cols] = (active * up).astype(BF16)
            gate_grad_ref[at, cols] = (
                grad * up * logistic * (1.0 + gate * (1.0 - logistic))
            ).astype(BF16)
            up_grad_ref[at, cols] = (grad * active).astype(BF16)

    sent(0)
    x_copy.wait()
    s_copy.wait()
    for j in others:
        pl.semaphore_signal(
            ready, inc=1, device_id=peer(j, 0), device_id_type=pl.DeviceIdType.MESH
        )
    piece = width // CHUNKS

    def to_replica(c, j):
        cols = pl.ds(c * piece, piece)
        theirs = pl.ds(lax.rem(d + j, replicas) * experts, experts)
        return remote(
            xbuf.at[theirs, :, cols],
            ubuf.at[pl.ds(j * experts, experts), :, cols],
            y_send.at[c, j - 1],
            y_recv.at[c, j - 1],
            peer(j, 0),
        )

    def to_expert(c, k):
        cols = pl.ds(c * piece, piece)
        return remote(
            xbuf.at[slot(d, lax.rem(e + k, experts)), :, cols],
            back_buf.at[k - 1, :, cols],
            z_send.at[c, k - 1],
            z_recv.at[c, k - 1],
            peer(0, k),
        )

    for c in range(CHUNKS + 2):
        if c < CHUNKS:
            cols = pl.ds(c * piece, piece)

            @pl.loop(0, blocks)
            def _(r):
                at = pl.ds(pl.multiple_of(r * height, height), height)
                back = lax.dot_general(
                    gate_grad_ref[at, :], gate_w[cols, :], LAST, preferred_element_type=F32
                ) + lax.dot_general(
                    up_grad_ref[at, :], up_w[cols, :], LAST, preferred_element_type=F32
                )
                xbuf[pl.ds(r * per_block, per_block), :, cols] = back.astype(BF16).reshape(
                    per_block, rows, piece
                )

            if c == 0 and replicas > 1:
                pl.semaphore_wait(ready, replicas - 1)
            for j in others:
                to_replica(c, j).start()
        if c >= 2:
            q = c - 2
            cols = pl.ds(q * piece, piece)
            own = pl.ds(d * experts, experts)
            total = xbuf[own, :, cols].astype(F32)
            for j in others:
                to_replica(q, j).wait_recv()
                total = total + ubuf[pl.ds(j * experts, experts), :, cols].astype(F32)
            xbuf[own, :, cols] = total.astype(BF16)
            for k in range(1, experts):
                to_expert(q, k).start()
    for c in range(CHUNKS):
        cols = pl.ds(c * piece, piece)
        back = xbuf[me, :, cols].astype(F32)
        for k in range(1, experts):
            to_expert(c, k).wait_recv()
            back = back + back_buf[k - 1, :, cols].astype(F32)
        own_up[:, cols] = (own_up[:, cols].astype(F32) + back).astype(BF16)
    for c in range(CHUNKS):
        for j in others:
            to_replica(c, j).wait_send()
        for k in range(1, experts):
            to_expert(c, k).wait_send()


def exchange(sizes, incoming, stash, weight, gate, up, down):
    _, replicas, experts = sizes
    groups = replicas * experts
    rows, width = stash.shape
    hid = gate.shape[1]
    total = groups * rows
    tile = min(256, hid)
    per_block = max(1, min(groups, 256 // rows))
    dma = pltpu.SemaphoreType.DMA
    vmem, anywhere = pl.BlockSpec(memory_space=pltpu.VMEM), pl.BlockSpec(memory_space=pl.ANY)
    shape = jax.ShapeDtypeStruct
    pre = pltpu.VMEM((hid // tile, groups // per_block, per_block * rows, tile), F32)
    tokens = pltpu.VMEM((groups, rows, width), BF16)
    return pl.pallas_call(
        functools.partial(exchange_kernel, sizes),
        out_shape=[shape((rows, width), BF16)]
        + [shape((total, hid), BF16)] * 3
        + [shape((groups, rows, width), BF16)] * 2,
        in_specs=[vmem] * 3 + [anywhere] * 3,
        out_specs=[vmem] * 4 + [anywhere] * 2,
        scratch_shapes=[
            tokens,
            tokens,
            pltpu.VMEM((groups, rows, 128), F32),
            pltpu.VMEM((max(1, experts - 1), rows, width), BF16),
            pltpu.VMEM(gate.shape, BF16),
            pltpu.VMEM(up.shape, BF16),
            pltpu.VMEM(down.shape, BF16),
            pre,
            pre,
            dma((3,)),
            dma((2,)),
            dma((1,)),
            dma((1,)),
            dma((groups - 1,)),
            dma((groups - 1,)),
            dma((2, 2, 2, groups)),
            dma((2, 2, max(1, replicas - 1), experts)),
            dma((2, 2, groups)),
            pltpu.SemaphoreType.REGULAR,
            dma((CHUNKS, max(1, replicas - 1))),
            dma((CHUNKS, max(1, replicas - 1))),
            dma((CHUNKS, max(1, experts - 1))),
            dma((CHUNKS, max(1, experts - 1))),
        ],
        compiler_params=pltpu.CompilerParams(
            collective_id=0, has_side_effects=True, vmem_limit_bytes=VMEM_LIMIT
        ),
        cost_estimate=pl.CostEstimate(
            flops=10 * total * width * hid, bytes_accessed=6 * width * hid, transcendentals=0
        ),
    )(incoming, stash, weight, gate, up, down)


def outer_kernel(lhs, *refs):
    half = len(refs) // 2
    for rhs, out in zip(refs[:half], refs[half:]):
        out[...] = lax.dot_general(lhs[...], rhs[...], FIRST, preferred_element_type=F32).astype(
            BF16
        )


def outer(lhs, tile, *rhs):
    total, height = lhs.shape
    out_width = rhs[0].shape[1]
    tile = min(tile, height)
    return pl.pallas_call(
        outer_kernel,
        grid=(height // tile,),
        in_specs=[pl.BlockSpec((total, tile), lambda i: (0, i))]
        + [pl.BlockSpec((total, out_width), lambda i: (0, 0))] * len(rhs),
        out_specs=[pl.BlockSpec((tile, out_width), lambda i: (i, 0))] * len(rhs),
        out_shape=[jax.ShapeDtypeStruct((height, out_width), BF16)] * len(rhs),
        compiler_params=pltpu.CompilerParams(vmem_limit_bytes=VMEM_LIMIT),
        cost_estimate=pl.CostEstimate(
            flops=2 * total * height * out_width * len(rhs),
            bytes_accessed=2 * len(rhs) * height * out_width,
            transcendentals=0,
        ),
    )(lhs, *rhs)


def per_device(sizes, incoming, stash, expert_ids, route_weight, w_gate, w_up, w_down):
    mbatch, tok_rows, width = stash.shape[1:]
    rows = mbatch * tok_rows
    named = expert_ids[0][..., None] == jnp.arange(128, dtype=jnp.int32)
    weight = jnp.sum(jnp.where(named, route_weight[0][..., None], 0.0), axis=2).reshape(rows, 128)
    outs = exchange(
        sizes,
        incoming[0].reshape(rows, width),
        stash[0].reshape(rows, width),
        weight,
        w_gate[0, 0],
        w_up[0, 0],
        w_down[0, 0],
    )
    input_grad, hidden, gate_grad, up_grad, tokens, scaled = outs
    tokens = tokens.reshape(-1, width)
    scaled = scaled.reshape(-1, width)
    grad_gate, grad_up = outer(tokens, 512, gate_grad, up_grad)
    (grad_down,) = outer(hidden, 256, scaled)
    return (
        input_grad.reshape(1, mbatch, tok_rows, width),
        grad_gate[None, None],
        grad_up[None, None],
        grad_down[None, None],
    )


def solution(mesh):
    sizes = tuple(mesh.shape[name] for name in ("section", "dp", "expert"))
    tokens = P("section", None, ("dp", "expert"), None)
    columns = P("section", "expert", None, "dp")
    rows = P("section", "expert", "dp", None)
    return jax.shard_map(
        functools.partial(per_device, sizes),
        mesh=mesh,
        in_specs=(tokens, tokens, tokens, tokens, columns, columns, rows),
        out_specs=(tokens, columns, columns, rows),
        check_vma=False,
    )
```

```python
import functools

import jax
import jax.numpy as jnp
from jax import lax
from jax.experimental import pallas as pl
from jax.experimental.pallas import tpu as pltpu
from jax.sharding import PartitionSpec as P

F32 = jnp.float32
BF16 = jnp.bfloat16
LAST = (((1,), (1,)), ((), ()))
FIRST = (((0,), (0,)), ((), ()))
VMEM_LIMIT = 60 * 1024 * 1024
CHUNKS = 7


def exchange_kernel(sizes, *refs):
    sections, replicas, experts = sizes
    (incoming, stash, weight, gate_hbm, up_hbm, down_hbm), refs = refs[:6], refs[6:]
    (own_up, hidden_ref, gate_grad_ref, up_grad_ref, x_out, s_out), refs = refs[:6], refs[6:]
    (xbuf, ubuf, wbuf, back_buf, gate_w, up_w, down_w, gate_pre, up_pre) = refs[:9]
    (load_sem, out_sem, shift_send, shift_recv, w_send, w_recv, zsend, dsend, recv) = refs[9:18]
    (ready, y_send, y_recv, z_send, z_recv) = refs[18:]
    groups, rows, width = xbuf.shape
    hid = gate_w.shape[1]
    tile = min(256, hid)
    tiles = hid // tile
    per_block = max(1, min(groups, 256 // rows))
    blocks = groups // per_block
    height = per_block * rows
    s, d, e = lax.axis_index("section"), lax.axis_index("dp"), lax.axis_index("expert")
    cut = (width // 128) * 17 // 28 * 128
    columns = (pl.ds(0, cut), pl.ds(cut, width - cut))

    def slot(replica, expert):
        return lax.rem(replica + replicas, replicas) * experts + jnp.clip(expert, 0, experts - 1)

    me = slot(d, e)
    loads = [
        pltpu.make_async_copy(src, dst, load_sem.at[i])
        for i, (src, dst) in enumerate(((gate_hbm, gate_w), (up_hbm, up_w), (down_hbm, down_w)))
    ]
    peers = [(j, k) for j in range(replicas) for k in range(experts) if j or k]

    def peer(j, k):
        return {"dp": lax.rem(d + j, replicas), "expert": lax.rem(e + k, experts)}

    before = {"section": lax.rem(s + sections - 1, sections)}
    after = {"section": lax.rem(s + 1, sections)}
    barrier = pltpu.get_barrier_semaphore()
    for target in [peer(j, k) for j, k in peers] + [before, after]:
        pl.semaphore_signal(barrier, inc=1, device_id=target, device_id_type=pl.DeviceIdType.MESH)
    xbuf[me] = stash[...]
    wbuf[me] = weight[...]
    pl.semaphore_wait(barrier, len(peers) + 2)

    def remote(src, dst, send, arrive, target):
        return pltpu.make_async_remote_copy(
            src_ref=src,
            dst_ref=dst,
            send_sem=send,
            recv_sem=arrive,
            device_id=target,
            device_id_type=pl.DeviceIdType.MESH,
        )

    bufs = (xbuf, ubuf)

    def along_z(a, c, block, way):
        ref = bufs[a].at[block, :, columns[c]]
        other = jnp.clip(e + 1 if way == 0 else e - 1, 0, experts - 1)
        return remote(ref, ref, zsend.at[a, c, way, block], recv.at[a, c, block], {"expert": other})

    def along_dp(a, c, expert, j):
        block = slot(d, expert)
        ref = bufs[a].at[block, :, columns[c]]
        at = jnp.clip(expert, 0, experts - 1)
        return remote(ref, ref, dsend.at[a, c, j - 1, at], recv.at[a, c, block], peer(j, 0))

    def arrived(a, c, block):
        ref = bufs[a].at[block, :, columns[c]]
        remote(ref, ref, zsend.at[a, c, 0, block], recv.at[a, c, block], peer(1, 0)).wait_recv()

    others = range(1, replicas)
    has = (e < experts - 1, e > 0)

    def both_ways(a, c, block):
        for way in range(2):
            pl.when(has[way])(lambda way=way: along_z(a, c, block, way).start())

    def first(a):
        for j in others:
            along_dp(a, 1, e, j).start()
        both_ways(a, 0, me)
        for j in others:
            along_dp(a, 0, e, j).start()
        both_ways(a, 1, me)

    def relay(a, c, replica, k, with_dp):
        for way, origin, there in ((0, e - k, e - k >= 0), (1, e + k, e + k < experts)):

            @pl.when(there)
            def _():
                block = slot(replica, origin)
                arrived(a, c, block)
                pl.when(has[way])(lambda: along_z(a, c, block, way).start())
                if with_dp:
                    for j in others:
                        along_dp(a, c, origin, j).start()

    def step(a, k):
        relay(a, 0, d, k, True)
        for j in others:
            if k == 1:
                arrived(a, 1, slot(d - j, e))
                both_ways(a, 1, slot(d - j, e))
            else:
                relay(a, 1, d - j, k - 1, False)
        relay(a, 1, d, k, False)

    def finish(a):
        for j in others:
            relay(a, 1, d - j, experts - 1, False)
            for expert in range(experts):
                arrived(a, 0, slot(d - j, expert))

    def sent(a):
        for c in range(2):
            for j in others:
                for expert in range(experts):
                    if c == 0:
                        along_dp(a, 0, expert, j).wait_send()
                if c == 1:
                    along_dp(a, 1, e, j).wait_send()
            for j in range(replicas if c == 1 else 1):
                for k in range(experts):
                    for way, origin, there in ((0, e - k, e - k >= 0), (1, e + k, e + k < experts)):

                        @pl.when(jnp.logical_and(there, has[way]))
                        def _():
                            along_z(a, c, slot(d - j, origin), way).wait_send()

    shift = remote(incoming, ubuf.at[me], shift_send.at[0], shift_recv.at[0], before)
    shift.start()
    first(0)
    weight_copies = []
    for n, (j, k) in enumerate(peers):
        copy = remote(wbuf.at[me], wbuf.at[me], w_send.at[n], w_recv.at[n], peer(j, k))
        copy.start()
        weight_copies.append(copy)
    for load in loads:
        load.start()
    shift.wait()
    own_up[...] = ubuf[me]
    first(1)
    for k in range(1, experts):
        step(0, k)
        if k > 1:
            step(1, k - 1)
    finish(0)
    x_copy = pltpu.make_async_copy(xbuf, x_out, out_sem.at[0])
    x_copy.start()
    loads[0].wait()
    loads[1].wait()

    def forward(lo, hi):
        @pl.loop(lo, hi)
        def _(h):
            cols = pl.ds(pl.multiple_of(h * tile, tile), tile)

            @pl.loop(0, blocks)
            def _(r):
                x = xbuf[pl.ds(r * per_block, per_block)].reshape(height, width)
                gate_pre[h, r] = jnp.dot(x, gate_w[:, cols], preferred_element_type=F32)
                up_pre[h, r] = jnp.dot(x, up_w[:, cols], preferred_element_type=F32)

    if tiles > 1:
        forward(0, tiles // 2)
    step(1, experts - 1)
    forward(tiles // 2, tiles)
    finish(1)
    for copy in weight_copies:
        copy.wait()
    sent(1)
    lane = lax.broadcasted_iota(jnp.int32, wbuf.shape[1:], 1)

    @pl.loop(0, groups)
    def _(g):
        own = jnp.sum(jnp.where(lane == e, wbuf[g], 0.0), axis=1, keepdims=True)
        ubuf[g] = (own * ubuf[g].astype(F32)).astype(BF16)

    s_copy = pltpu.make_async_copy(ubuf, s_out, out_sem.at[1])
    s_copy.start()
    loads[2].wait()

    @pl.loop(0, tiles)
    def _(h):
        cols = pl.ds(pl.multiple_of(h * tile, tile), tile)

        @pl.loop(0, blocks)
        def _(r):
            at = pl.ds(pl.multiple_of(r * height, height), height)
            scaled = ubuf[pl.ds(r * per_block, per_block)].reshape(height, width)
            grad = lax.dot_general(scaled, down_w[cols, :], LAST, preferred_element_type=F32)
            gate, up = gate_pre[h, r], up_pre[h, r]
            logistic = jax.nn.sigmoid(gate)
            active = gate * logistic
            hidden_ref[at, cols] = (active * up).astype(BF16)
            gate_grad_ref[at, cols] = (
                grad * up * logistic * (1.0 + gate * (1.0 - logistic))
            ).astype(BF16)
            up_grad_ref[at, cols] = (grad * active).astype(BF16)

    sent(0)
    x_copy.wait()
    s_copy.wait()
    for j in others:
        pl.semaphore_signal(
            ready, inc=1, device_id=peer(j, 0), device_id_type=pl.DeviceIdType.MESH
        )
    piece = width // CHUNKS

    def to_replica(c, j):
        cols = pl.ds(c * piece, piece)
        theirs = pl.ds(lax.rem(d + j, replicas) * experts, experts)
        return remote(
            xbuf.at[theirs, :, cols],
            ubuf.at[pl.ds(j * experts, experts), :, cols],
            y_send.at[c, j - 1],
            y_recv.at[c, j - 1],
            peer(j, 0),
        )

    def to_expert(c, k):
        cols = pl.ds(c * piece, piece)
        return remote(
            xbuf.at[slot(d, lax.rem(e + k, experts)), :, cols],
            back_buf.at[k - 1, :, cols],
            z_send.at[c, k - 1],
            z_recv.at[c, k - 1],
            peer(0, k),
        )

    for c in range(CHUNKS + 2):
        if c < CHUNKS:
            cols = pl.ds(c * piece, piece)

            @pl.loop(0, blocks)
            def _(r):
                at = pl.ds(pl.multiple_of(r * height, height), height)
                back = lax.dot_general(
                    gate_grad_ref[at, :], gate_w[cols, :], LAST, preferred_element_type=F32
                ) + lax.dot_general(
                    up_grad_ref[at, :], up_w[cols, :], LAST, preferred_element_type=F32
                )
                xbuf[pl.ds(r * per_block, per_block), :, cols] = back.astype(BF16).reshape(
                    per_block, rows, piece
                )

            if c == 0 and replicas > 1:
                pl.semaphore_wait(ready, replicas - 1)
            for j in others:
                to_replica(c, j).start()
        if c >= 2:
            q = c - 2
            cols = pl.ds(q * piece, piece)
            own = pl.ds(d * experts, experts)
            total = xbuf[own, :, cols].astype(F32)
            for j in others:
                to_replica(q, j).wait_recv()
                total = total + ubuf[pl.ds(j * experts, experts), :, cols].astype(F32)
            xbuf[own, :, cols] = total.astype(BF16)
            for k in range(1, experts):
                to_expert(q, k).start()
    for c in range(CHUNKS):
        cols = pl.ds(c * piece, piece)
        back = xbuf[me, :, cols].astype(F32)
        for k in range(1, experts):
            to_expert(c, k).wait_recv()
            back = back + back_buf[k - 1, :, cols].astype(F32)
        own_up[:, cols] = (own_up[:, cols].astype(F32) + back).astype(BF16)
    for c in range(CHUNKS):
        for j in others:
            to_replica(c, j).wait_send()
        for k in range(1, experts):
            to_expert(c, k).wait_send()


def exchange(sizes, incoming, stash, weight, gate, up, down):
    _, replicas, experts = sizes
    groups = replicas * experts
    rows, width = stash.shape
    hid = gate.shape[1]
    total = groups * rows
    tile = min(256, hid)
    per_block = max(1, min(groups, 256 // rows))
    dma = pltpu.SemaphoreType.DMA
    vmem, anywhere = pl.BlockSpec(memory_space=pltpu.VMEM), pl.BlockSpec(memory_space=pl.ANY)
    shape = jax.ShapeDtypeStruct
    pre = pltpu.VMEM((hid // tile, groups // per_block, per_block * rows, tile), F32)
    tokens = pltpu.VMEM((groups, rows, width), BF16)
    return pl.pallas_call(
        functools.partial(exchange_kernel, sizes),
        out_shape=[shape((rows, width), BF16)]
        + [shape((total, hid), BF16)] * 3
        + [shape((groups, rows, width), BF16)] * 2,
        in_specs=[vmem] * 3 + [anywhere] * 3,
        out_specs=[vmem] * 4 + [anywhere] * 2,
        scratch_shapes=[
            tokens,
            tokens,
            pltpu.VMEM((groups, rows, 128), F32),
            pltpu.VMEM((max(1, experts - 1), rows, width), BF16),
            pltpu.VMEM(gate.shape, BF16),
            pltpu.VMEM(up.shape, BF16),
            pltpu.VMEM(down.shape, BF16),
            pre,
            pre,
            dma((3,)),
            dma((2,)),
            dma((1,)),
            dma((1,)),
            dma((groups - 1,)),
            dma((groups - 1,)),
            dma((2, 2, 2, groups)),
            dma((2, 2, max(1, replicas - 1), experts)),
            dma((2, 2, groups)),
            pltpu.SemaphoreType.REGULAR,
            dma((CHUNKS, max(1, replicas - 1))),
            dma((CHUNKS, max(1, replicas - 1))),
            dma((CHUNKS, max(1, experts - 1))),
            dma((CHUNKS, max(1, experts - 1))),
        ],
        compiler_params=pltpu.CompilerParams(
            collective_id=0, has_side_effects=True, vmem_limit_bytes=VMEM_LIMIT
        ),
        cost_estimate=pl.CostEstimate(
            flops=10 * total * width * hid, bytes_accessed=6 * width * hid, transcendentals=0
        ),
    )(incoming, stash, weight, gate, up, down)


def outer_kernel(lhs, *refs):
    half = len(refs) // 2
    for rhs, out in zip(refs[:half], refs[half:]):
        out[...] = lax.dot_general(lhs[...], rhs[...], FIRST, preferred_element_type=F32).astype(
            BF16
        )


def outer(lhs, tile, *rhs):
    total, height = lhs.shape
    out_width = rhs[0].shape[1]
    tile = min(tile, height)
    return pl.pallas_call(
        outer_kernel,
        grid=(height // tile,),
        in_specs=[pl.BlockSpec((total, tile), lambda i: (0, i))]
        + [pl.BlockSpec((total, out_width), lambda i: (0, 0))] * len(rhs),
        out_specs=[pl.BlockSpec((tile, out_width), lambda i: (i, 0))] * len(rhs),
        out_shape=[jax.ShapeDtypeStruct((height, out_width), BF16)] * len(rhs),
        compiler_params=pltpu.CompilerParams(vmem_limit_bytes=VMEM_LIMIT),
        cost_estimate=pl.CostEstimate(
            flops=2 * total * height * out_width * len(rhs),
            bytes_accessed=2 * len(rhs) * height * out_width,
            transcendentals=0,
        ),
    )(lhs, *rhs)


def per_device(sizes, incoming, stash, expert_ids, route_weight, w_gate, w_up, w_down):
    mbatch, tok_rows, width = stash.shape[1:]
    rows = mbatch * tok_rows
    named = expert_ids[0][..., None] == jnp.arange(128, dtype=jnp.int32)
    weight = jnp.sum(jnp.where(named, route_weight[0][..., None], 0.0), axis=2).reshape(rows, 128)
    outs = exchange(
        sizes,
        incoming[0].reshape(rows, width),
        stash[0].reshape(rows, width),
        weight,
        w_gate[0, 0],
        w_up[0, 0],
        w_down[0, 0],
    )
    input_grad, hidden, gate_grad, up_grad, tokens, scaled = outs
    tokens = tokens.reshape(-1, width)
    scaled = scaled.reshape(-1, width)
    grad_gate, grad_up = outer(tokens, 512, gate_grad, up_grad)
    (grad_down,) = outer(hidden, 256, scaled)
    return (
        input_grad.reshape(1, mbatch, tok_rows, width),
        grad_gate[None, None],
        grad_up[None, None],
        grad_down[None, None],
    )


def solution(mesh):
    sizes = tuple(mesh.shape[name] for name in ("section", "dp", "expert"))
    tokens = P("section", None, ("dp", "expert"), None)
    columns = P("section", "expert", None, "dp")
    rows = P("section", "expert", "dp", None)
    return jax.shard_map(
        functools.partial(per_device, sizes),
        mesh=mesh,
        in_specs=(tokens, tokens, tokens, tokens, columns, columns, rows),
        out_specs=(tokens, columns, columns, rows),
        check_vma=False,
    )
```
